1024 devices in a mesh: dp: 128 (over z, x), tm: 8 (over y, core).
Axes of the slice: x: 4, y: 4, z: 32, core: 2. Of those that a mesh axis runs over, the one named last changes fastest.
Arguments:
- frames: bfloat16 [4096, 96, 1024], P(('dp', 'tm')), may hold values from -6 to 6
- texts: bfloat16 [8192, 1024], P(('dp', 'tm')), may hold values from -6 to 6
- w_query: bfloat16 [1024, 1024], replicated, may hold values from -0.1875 to 0.1875
- w_key: bfloat16 [1024, 1024], replicated, may hold values from -0.1875 to 0.1875
- w_value: bfloat16 [1024, 1024], replicated, may hold values from -0.1875 to 0.1875
- w_out: bfloat16 [1024, 1024], replicated, may hold values from -0.1875 to 0.1875
- frame_counts: int32 [4096], P(('dp', 'tm')), may hold values from 1 to 96, as said below
- clip_pos: int32 [4096], P(('dp', 'tm')), may hold values from 0 to 191
Outputs:
- similar: float32 [4096, 3, 64], P(('dp', 'tm'))
- clip_loss: float32 [4096], P(('dp', 'tm'))
- text_lse: float32 [8192], P(('dp', 'tm'))
The draws below stay inside these ranges and needn't reach their ends.
Inputs may be any that keep to these rules, and one draw needn't show every extreme that they name: `frame_counts`: some clip has all 96 frames valid and some clip only one.
All inputs are finite; a program needn't handle non-finite values.
Results may differ from the reference program's by a relative error of at most 0.0061.
Values may be sent and summed in bfloat16 or wider, within the bound.
No kernel may reach another device: no remote copies, remote signals or barrier semaphores. Data moves between devices by JAX's collectives and lax.ppermute only.
A program may use at most 32 MiB of HBM per device.

```python
import math
import jax
import jax.numpy as jnp
from jax import lax

D = 1024
FRAMES = 96
TB = 64
HOPS = 2
CLIP_BLOCK = 32
CLIPS = 4096
TEXTS = 8192
BAND = 192
N_DP = 128


def draw_frame_counts(key, part):
    key = jax.random.fold_in(key, 7)
    key_count, key_order = jax.random.split(key)
    counts = jax.random.randint(key_count, (CLIPS,), 1, FRAMES + 1)
    shuffled = jax.random.permutation(key_order, CLIPS)
    counts = counts.at[shuffled[0]].set(FRAMES)
    counts = counts.at[shuffled[1]].set(1)
    return counts.astype(jnp.int32)


def set_ends(array, rng, smallest, top_value):
    longest = array.shape.index(max(array.shape))
    spots = []
    for shift in (0, 1):
        where = [jax.random.randint(jax.random.fold_in(rng, axis), (), 0, length) for axis, length in enumerate(array.shape)]
        where[longest] = (where[longest] + shift) % array.shape[longest]
        spots.append(tuple(where))
    return array.at[spots[0]].set(smallest).at[spots[1]].set(top_value)


def block_scale(own_key, shape, shards, least, largest):
    def one(dim, parts):
        heights = jax.random.uniform(jax.random.fold_in(jax.random.fold_in(own_key, 6), dim), (parts,), jnp.float32, least / len(shards), largest / len(shards))
        return jnp.repeat(jnp.exp(heights), shape[dim] // parts).reshape((-1,) + (1,) * (len(shape) - dim - 1))

    factor_of = one(*shards[0])
    for cut in shards[1:]:
        factor_of = factor_of * one(*cut)
    return factor_of


def gaussian(own_key, extent, spread, reach, shards=(), held_as=jnp.bfloat16):
    gain = block_scale(own_key, extent, shards, -0.22, 0.18) if shards else 1.0
    result = jax.random.normal(own_key, extent, jnp.float32) * spread * gain
    return jnp.minimum(jnp.maximum(result, -reach), reach).astype(held_as)


def setup_inputs(seed: int = 0) -> dict:
    key_of = jax.random.split(jax.random.key(seed), 9)
    return {
        "frames": gaussian(key_of[0], (CLIPS, FRAMES, D), 1.0, 6.0, ((0, 1024),)),
        "texts": gaussian(key_of[1], (TEXTS, D), 1.0, 6.0, ((0, 1024),)),
        "w_query": gaussian(key_of[2], (D, D), D ** -0.5, 0.1875),
        "w_key": gaussian(key_of[3], (D, D), D ** -0.5, 0.1875),
        "w_value": gaussian(key_of[4], (D, D), D ** -0.5, 0.1875),
        "w_out": gaussian(key_of[5], (D, D), D ** -0.5, 0.1875),
        "frame_counts": draw_frame_counts(jax.random.fold_in(key_of[8], 71), 0),
        "clip_pos": set_ends(jax.random.randint(key_of[7], (CLIPS,), 0, BAND), jax.random.fold_in(key_of[7], 1), 0, BAND - 1).astype(jnp.int32),
    }


LOGIT_SCALE = 32.0
EPSILON = 1e-06

def cosine_scaled(pooled, text_rows):
    inner = lax.optimization_barrier(jnp.sum(pooled * text_rows, axis=-1))
    pooled_sq = lax.optimization_barrier(jnp.sum(pooled * pooled, axis=-1))
    text_sq = lax.optimization_barrier(jnp.sum(text_rows * text_rows, axis=-1))
    return LOGIT_SCALE * inner / jnp.sqrt((pooled_sq + EPSILON) * (text_sq + EPSILON))

def reference(frames, texts, w_query, w_key, w_value, w_out, frame_counts, clip_pos):
    queries = jnp.dot(texts, w_query, preferred_element_type=jnp.float32).astype(jnp.bfloat16)
    frame_flat = frames.reshape(-1, D)
    key_rows = jnp.dot(frame_flat, w_key, preferred_element_type=jnp.float32).astype(jnp.bfloat16).reshape(CLIPS, FRAMES, D)
    value_rows = jnp.dot(frame_flat, w_value, preferred_element_type=jnp.float32).astype(jnp.bfloat16).reshape(CLIPS, FRAMES, D)
    frame_index = jnp.arange(FRAMES, dtype=jnp.int32)

    def one_block(block):
        start = (block * CLIP_BLOCK).astype(jnp.int32)
        keys_here = lax.dynamic_slice_in_dim(key_rows, start, CLIP_BLOCK, 0)
        values_here = lax.dynamic_slice_in_dim(value_rows, start, CLIP_BLOCK, 0)
        counts_here = lax.dynamic_slice_in_dim(frame_counts, start, CLIP_BLOCK, 0)
        pos_here = lax.dynamic_slice_in_dim(clip_pos, start, CLIP_BLOCK, 0)
        band_query = []
        band_text = []
        for step in range(HOPS + 1):
            source = ((block - step) % N_DP * TB).astype(jnp.int32)
            band_query.append(lax.dynamic_slice_in_dim(queries, source, TB, 0))
            band_text.append(lax.dynamic_slice_in_dim(texts, source, TB, 0))
        band_query = jnp.concatenate(band_query, axis=0)
        band_text = jnp.concatenate(band_text, axis=0).astype(jnp.float32)
        scores = jnp.einsum('tk,cfk->ctf', band_query.astype(jnp.float32), keys_here.astype(jnp.float32)) / math.sqrt(D)
        valid_mask = frame_index[None, None, :] < counts_here[:, None, None]
        frame_weights = jnp.where(valid_mask, jnp.exp(scores), 0.0)
        weight_sum = lax.optimization_barrier(jnp.sum(frame_weights, axis=-1))
        rounded = lax.optimization_barrier(frame_weights.astype(jnp.bfloat16))
        weighted = jnp.einsum('ctf,cfk->ctk', rounded.astype(jnp.float32), values_here.astype(jnp.float32))
        attended = (weighted / weight_sum[..., None]).astype(jnp.bfloat16)
        pooled = jnp.dot(attended.reshape(-1, D), w_out, preferred_element_type=jnp.float32).reshape(CLIP_BLOCK, BAND, D)
        similar = cosine_scaled(pooled, band_text[None])
        exp_sims = jnp.exp(similar)
        picked = jnp.take_along_axis(similar, pos_here[:, None], axis=1)[:, 0]
        clip_loss = jnp.log(lax.optimization_barrier(jnp.sum(exp_sims, axis=-1))) - picked
        text_terms = lax.optimization_barrier(jnp.sum(exp_sims, axis=0))
        return (similar.reshape(CLIP_BLOCK, HOPS + 1, TB), clip_loss, text_terms.reshape(HOPS + 1, TB))
    block_ids = jnp.arange(N_DP, dtype=jnp.int32)
    similar, clip_loss, text_terms = lax.map(one_block, block_ids)
    similar = similar.reshape(CLIPS, HOPS + 1, TB)
    clip_loss = clip_loss.reshape(CLIPS)
    totals = jnp.zeros((N_DP, TB), jnp.float32)
    for step in range(HOPS + 1):
        totals = totals + jnp.roll(text_terms[:, step], -step, axis=0)
    text_lse = jnp.log(totals).reshape(TEXTS)
    return (similar, clip_loss, text_lse)
```

```python
import jax
import jax.numpy as jnp
from jax import lax
from jax.experimental import pallas as pl
from jax.experimental.pallas import tpu as pltpu
from jax.sharding import PartitionSpec as P

HOPS = 2
RING = 4
LOGIT_SCALE = 32.0
EPSILON = 1e-06
BOTH = ("dp", "tm")
F32 = jnp.float32
BF16 = jnp.bfloat16
ROWS = (((1,), (1,)), ((), ()))


def ring_groups(dp_count, tm_count):
    width = RING * tm_count
    return [list(range(g * width, (g + 1) * width)) for g in range(dp_count // RING)]


def moved(value, blocks):
    count = lax.axis_size("dp")
    pairs = [(source, (source + blocks) % count) for source in range(count)]
    return lax.ppermute(value, "dp", pairs)


def split_bf16(value):
    high = value.astype(BF16)
    return high, (value - high.astype(F32)).astype(BF16)


def score_kernel(
    place_ref, counts_ref, pos_ref, text_ref, key_ref, value_ref, gram_ref,
    similar_ref, loss_ref, terms_ref,
):
    clips, frames = gram_ref.shape[0], gram_ref.shape[1]
    texts = text_ref.shape[0]
    block = texts // RING
    place = place_ref[0]
    text = text_ref[...]
    scores = lax.dot_general(key_ref[...], text, ROWS, preferred_element_type=F32)
    inner_all = lax.dot_general(value_ref[...], text, ROWS, preferred_element_type=F32)
    text_wide = text.astype(F32)
    text_sq = jnp.sum((text_wide * text_wide).reshape(texts, -1, 128).sum(1).T, axis=0, keepdims=True)
    lane = lax.broadcasted_iota(jnp.int32, (1, texts), 1)
    hop = (place - lane // block + RING) % RING
    band_index = hop * block + lane % block
    in_band = hop <= HOPS
    frame_index = lax.broadcasted_iota(jnp.int32, (frames, texts), 0)
    terms = jnp.zeros((1, texts), F32)
    for clip in range(clips):
        rows = slice(clip * frames, (clip + 1) * frames)
        valid = frame_index < counts_ref[clip]
        score = jnp.where(valid, scores[rows], -jnp.inf)
        weights = jnp.exp(score - jnp.max(score, axis=0, keepdims=True))
        weights = weights * (1.0 / jnp.sum(weights, axis=0, keepdims=True))
        inner = jnp.sum(weights * inner_all[rows], axis=0, keepdims=True)
        w_high, w_low = split_bf16(weights)
        g_high, g_low = split_bf16(gram_ref[clip])
        mixed = (
            jnp.dot(g_high, w_high, preferred_element_type=F32)
            + jnp.dot(g_high, w_low, preferred_element_type=F32)
            + jnp.dot(g_low, w_high, preferred_element_type=F32)
        )
        pooled_sq = jnp.maximum(jnp.sum(weights * mixed, axis=0, keepdims=True), 0.0)
        similar = LOGIT_SCALE * inner / jnp.sqrt((pooled_sq + EPSILON) * (text_sq + EPSILON))
        for j in range(HOPS + 1):
            at = (place - j + RING) % RING
            part = similar[:, :block]
            for x in range(1, RING):
                part = jnp.where(at == x, similar[:, x * block:(x + 1) * block], part)
            similar_ref[clip, j:j + 1, :] = part
        exp_sims = jnp.where(in_band, jnp.exp(similar), 0.0)
        picked = jnp.sum(jnp.where(band_index == pos_ref[clip], similar, 0.0), axis=1, keepdims=True)
        total = jnp.sum(exp_sims, axis=1, keepdims=True)
        loss_ref[clip:clip + 1, :] = jnp.broadcast_to(jnp.log(total) - picked, (1, 128))
        terms = terms + exp_sims
    terms_ref[...] = jnp.broadcast_to(terms, terms_ref.shape)


def local(frames, texts, w_query, w_key, w_value, w_out, frame_counts, clip_pos):
    clips, frame_total, width = frames.shape
    slice_rows = texts.shape[0]
    tm_count = lax.axis_size("tm")
    groups = ring_groups(lax.axis_size("dp"), tm_count)
    peers = RING * tm_count
    block_rows = slice_rows * tm_count
    place = lax.axis_index("dp") % RING

    before = moved(texts, RING)
    target = jnp.arange(RING, dtype=jnp.int32)[:, None, None, None]
    outgoing = jnp.where(target >= place, texts[None, None], before[None, None])
    outgoing = jnp.broadcast_to(outgoing, (RING, tm_count, slice_rows, width))
    band_text = lax.all_to_all(
        outgoing.reshape(peers, slice_rows, width), BOTH, 0, 0, axis_index_groups=groups, tiled=True
    ).reshape(peers * slice_rows, width)

    flat = frames.reshape(-1, width)
    key_rows = jnp.dot(flat, w_key, preferred_element_type=F32).astype(BF16)
    key_rows = lax.dot_general(key_rows, w_query, ROWS, preferred_element_type=F32)
    key_rows = (key_rows * (width ** -0.5)).astype(BF16)
    value_rows = jnp.dot(flat, w_value, preferred_element_type=F32).astype(BF16)
    value_rows = jnp.dot(value_rows, w_out, preferred_element_type=F32).astype(BF16)
    by_clip = value_rows.reshape(clips, frame_total, width)
    gram = jnp.einsum("cfk,cgk->cfg", by_clip, by_clip, preferred_element_type=F32)

    smem = pl.BlockSpec(memory_space=pltpu.SMEM)
    vmem = pl.BlockSpec(memory_space=pltpu.VMEM)
    similar, loss, terms = pl.pallas_call(
        score_kernel,
        in_specs=[smem] * 3 + [vmem] * 4,
        out_specs=[vmem] * 3,
        out_shape=[
            jax.ShapeDtypeStruct((clips, HOPS + 1, block_rows), F32),
            jax.ShapeDtypeStruct((clips, 128), F32),
            jax.ShapeDtypeStruct((peers, peers * slice_rows), F32),
        ],
        compiler_params=pltpu.CompilerParams(vmem_limit_bytes=24 * 1024 * 1024),
        cost_estimate=pl.CostEstimate(flops=500_000_000, bytes_accessed=3_000_000, transcendentals=120_000),
    )(place.reshape(1), frame_counts, clip_pos, band_text, key_rows, value_rows, gram)

    met = lax.all_to_all(terms, BOTH, 0, 0, axis_index_groups=groups, tiled=True)
    home = (place * tm_count + lax.axis_index("tm")) * slice_rows
    met = lax.dynamic_slice_in_dim(met, home, slice_rows, axis=1).reshape(RING, tm_count, slice_rows)
    own = (jnp.arange(RING, dtype=jnp.int32) >= place)[:, None, None]
    own_sum = jnp.sum(jnp.where(own, met, 0.0), axis=(0, 1))
    before_sum = jnp.sum(jnp.where(own, 0.0, met), axis=(0, 1))
    text_lse = jnp.log(own_sum + moved(before_sum, -RING))
    return (similar, loss[:, 0], text_lse)


def solution(mesh):
    in_specs = (
        P(BOTH, None, None), P(BOTH, None), P(), P(), P(), P(), P(BOTH), P(BOTH),
    )
    out_specs = (P(BOTH, None, None), P(BOTH), P(BOTH))
    return jax.shard_map(local, mesh=mesh, in_specs=in_specs, out_specs=out_specs, check_vma=False)
```

```python
import jax
import jax.numpy as jnp
from jax import lax
from jax.experimental import pallas as pl
from jax.experimental.pallas import tpu as pltpu
from jax.sharding import PartitionSpec as P

HOPS = 2
PAIR = 2
LOGIT_SCALE = 32.0
EPSILON = 1e-06
SLICE = 8
BOTH = ("dp", "tm")
F32 = jnp.float32
BF16 = jnp.bfloat16
ROWS = (((1,), (1,)), ((), ()))


def pair_groups(dp_count, tm_count):
    width = PAIR * tm_count
    return [list(range(g * width, (g + 1) * width)) for g in range(dp_count // PAIR)]


def moved(value, blocks):
    count = lax.axis_size("dp")
    pairs = [(source, (source + blocks) % count) for source in range(count)]
    return lax.ppermute(value, "dp", pairs)


def split_bf16(value):
    high = value.astype(BF16)
    return high, (value - high.astype(F32)).astype(BF16)


def project_kernel(
    frames_hbm, key_hbm, query_hbm, value_hbm, out_hbm,
    key_ref, value_ref, gram_ref,
    frames_ref, value_weight, out_weight, key_weight, query_weight, rows_ref, sems,
):
    clips, count = gram_ref.shape[0], gram_ref.shape[1]
    scale = frames_ref.shape[1] ** -0.5
    loads = [
        pltpu.make_async_copy(source, held, sems.at[at])
        for at, (source, held) in enumerate((
            (frames_hbm, frames_ref), (value_hbm, value_weight), (out_hbm, out_weight),
            (key_hbm, key_weight), (query_hbm, query_weight),
        ))
    ]
    for load in loads:
        load.start()
    loads[0].wait()
    loads[1].wait()
    rows_ref[...] = jnp.dot(frames_ref[...], value_weight[...], preferred_element_type=F32).astype(BF16)
    loads[2].wait()
    value_ref[...] = jnp.dot(rows_ref[...], out_weight[...], preferred_element_type=F32).astype(BF16)
    loads[3].wait()
    rows_ref[...] = jnp.dot(frames_ref[...], key_weight[...], preferred_element_type=F32).astype(BF16)
    for clip in range(clips):
        own = value_ref[clip * count:(clip + 1) * count, :]
        gram_ref[clip] = lax.dot_general(own, own, ROWS, preferred_element_type=F32)
    loads[4].wait()
    keys = lax.dot_general(rows_ref[...], query_weight[...], ROWS, preferred_element_type=F32)
    key_ref[...] = (keys * scale).astype(BF16)


def score_kernel(
    place_ref, counts_ref, pos_ref, text_ref, key_ref, value_ref, gram_ref,
    similar_ref, loss_ref, terms_ref,
):
    clips, frames = gram_ref.shape[0], gram_ref.shape[1]
    texts = text_ref.shape[0]
    block = texts // (2 * PAIR)
    place = place_ref[0]
    text = text_ref[...]
    scores = lax.dot_general(key_ref[...], text, ROWS, preferred_element_type=F32)
    inner_all = lax.dot_general(value_ref[...], text, ROWS, preferred_element_type=F32)
    text_wide = text.astype(F32)
    sq_high, sq_low = split_bf16(text_wide * text_wide)
    ones = jnp.ones((8, text.shape[1]), BF16)
    text_sq = lax.dot_general(ones, sq_high, ROWS, preferred_element_type=F32)
    text_sq = (text_sq + lax.dot_general(ones, sq_low, ROWS, preferred_element_type=F32))[:1]
    frame_index = lax.broadcasted_iota(jnp.int32, (frames, texts), 0)
    clip_index = lax.broadcasted_iota(jnp.int32, (clips, texts), 0)
    inner = jnp.zeros((clips, texts), F32)
    pooled_sq = jnp.zeros((clips, texts), F32)
    position = jnp.zeros((clips, texts), jnp.int32)
    for clip in range(clips):
        rows = slice(clip * frames, (clip + 1) * frames)
        valid = frame_index < counts_ref[clip]
        score = jnp.where(valid, scores[rows], -jnp.inf)
        weights = jnp.exp(score - jnp.max(score, axis=0, keepdims=True))
        weights = weights * (1.0 / jnp.sum(weights, axis=0, keepdims=True))
        w_high, w_low = split_bf16(weights)
        g_high, g_low = split_bf16(gram_ref[clip])
        mixed = (
            jnp.dot(g_high, w_high, preferred_element_type=F32)
            + jnp.dot(g_high, w_low, preferred_element_type=F32)
            + jnp.dot(g_low, w_high, preferred_element_type=F32)
        )
        here = clip_index == clip
        inner = jnp.where(here, jnp.sum(weights * inner_all[rows], axis=0, keepdims=True), inner)
        pooled_sq = jnp.where(here, jnp.sum(weights * mixed, axis=0, keepdims=True), pooled_sq)
        position = jnp.where(here, pos_ref[clip], position)
    pooled_sq = jnp.maximum(pooled_sq, 0.0)
    similar = LOGIT_SCALE * inner / jnp.sqrt((pooled_sq + EPSILON) * (text_sq + EPSILON))
    lane = lax.broadcasted_iota(jnp.int32, (clips, texts), 1)
    older = lane // SLICE % 2
    hop = place - lane // (2 * block) + 2 * older
    in_block = lane // (2 * SLICE) * SLICE % block + lane % SLICE
    exp_sims = jnp.where((hop >= 0) & (hop <= HOPS), jnp.exp(similar), 0.0)
    terms_ref[...] = jnp.sum(exp_sims, axis=0, keepdims=True)
    similar_ref[...] = similar
    hit = (hop >= 0) & (hop <= HOPS) & (hop * block + in_block == position)
    picked = jnp.sum(jnp.where(hit, similar, 0.0), axis=1, keepdims=True)
    total = jnp.sum(exp_sims, axis=1, keepdims=True)
    loss_ref[...] = jnp.broadcast_to(jnp.log(total) - picked, loss_ref.shape)


def local(frames, texts, w_query, w_key, w_value, w_out, frame_counts, clip_pos):
    clips, frame_total, width = frames.shape
    slice_rows = texts.shape[0]
    tm_count = lax.axis_size("tm")
    groups = pair_groups(lax.axis_size("dp"), tm_count)
    peers = PAIR * tm_count
    block_rows = slice_rows * tm_count
    place = lax.axis_index("dp") % PAIR

    both = jnp.concatenate([texts, moved(texts, 2)], axis=0)
    smem = pl.BlockSpec(memory_space=pltpu.SMEM)
    vmem = pl.BlockSpec(memory_space=pltpu.VMEM)
    rows = clips * frame_total
    key_rows, value_rows, gram = pl.pallas_call(
        project_kernel,
        in_specs=[pl.BlockSpec(memory_space=pltpu.HBM)] * 5,
        out_specs=[vmem] * 3,
        out_shape=[
            jax.ShapeDtypeStruct((rows, width), BF16),
            jax.ShapeDtypeStruct((rows, width), BF16),
            jax.ShapeDtypeStruct((clips, frame_total, frame_total), F32),
        ],
        scratch_shapes=[
            pltpu.VMEM((rows, width), BF16),
            *[pltpu.VMEM((width, width), BF16)] * 4,
            pltpu.VMEM((rows, width), BF16),
            pltpu.SemaphoreType.DMA((5,)),
        ],
        compiler_params=pltpu.CompilerParams(vmem_limit_bytes=52 * 1024 * 1024),
        cost_estimate=pl.CostEstimate(
            flops=8 * rows * width * width, bytes_accessed=8 * width * width, transcendentals=0
        ),
    )(frames.reshape(rows, width), w_key, w_query, w_value, w_out)

    band_text = lax.all_to_all(
        jnp.broadcast_to(both[None], (peers, 2 * slice_rows, width)),
        BOTH, 0, 0, axis_index_groups=groups, tiled=True,
    ).reshape(2 * peers * slice_rows, width)

    similar, loss, terms = pl.pallas_call(
        score_kernel,
        in_specs=[smem] * 3 + [vmem] * 4,
        out_specs=[vmem] * 3,
        out_shape=[
            jax.ShapeDtypeStruct((clips, 2 * peers * slice_rows), F32),
            jax.ShapeDtypeStruct((clips, 128), F32),
            jax.ShapeDtypeStruct((1, 2 * peers * slice_rows), F32),
        ],
        compiler_params=pltpu.CompilerParams(vmem_limit_bytes=24 * 1024 * 1024),
        cost_estimate=pl.CostEstimate(flops=500_000_000, bytes_accessed=3_000_000, transcendentals=120_000),
    )(place.reshape(1), frame_counts, clip_pos, band_text, key_rows, value_rows, gram)

    beyond = moved(terms, -2)
    lane = lax.broadcasted_iota(jnp.int32, terms.shape, 1)
    met = jnp.where(lane // slice_rows % 2 == 0, terms, beyond)
    similar, loss, met = lax.optimization_barrier((similar, loss, met))
    met = jnp.broadcast_to(met[None], (peers,) + met.shape)
    met = lax.all_to_all(met, BOTH, 0, 0, axis_index_groups=groups, tiled=True)
    home = (place * tm_count + lax.axis_index("tm")) * 2 * slice_rows
    met = lax.dynamic_slice_in_dim(jnp.sum(met, axis=(0, 1)), home, 2 * slice_rows)
    text_lse = jnp.log(met[:slice_rows] + met[slice_rows:])

    similar = similar.reshape(clips, PAIR, tm_count, 2, slice_rows)

    def part(which, older):
        return similar[:, which, :, older, :].reshape(clips, block_rows)

    first = place == 0
    by_hop = [
        jnp.where(first, part(0, 0), part(1, 0)),
        jnp.where(first, part(1, 1), part(0, 0)),
        jnp.where(first, part(0, 1), part(1, 1)),
    ]
    return (jnp.stack(by_hop, axis=1), loss[:, 0], text_lse)


def solution(mesh):
    in_specs = (
        P(BOTH, None, None), P(BOTH, None), P(), P(), P(), P(), P(BOTH), P(BOTH),
    )
    out_specs = (P(BOTH, None, None), P(BOTH), P(BOTH))
    return jax.shard_map(local, mesh=mesh, in_specs=in_specs, out_specs=out_specs, check_vma=False)
```

```python
import jax
import jax.numpy as jnp
from jax import lax
from jax.experimental import pallas as pl
from jax.experimental.pallas import tpu as pltpu
from jax.sharding import PartitionSpec as P

HOPS = 2
PAIR = 2
LOGIT_SCALE = 32.0
EPSILON = 1e-06
SLICE = 8
BOTH = ("dp", "tm")
F32 = jnp.float32
BF16 = jnp.bfloat16
ROWS = (((1,), (1,)), ((), ()))


def pair_groups(dp_count, tm_count):
    width = PAIR * tm_count
    return [list(range(g * width, (g + 1) * width)) for g in range(dp_count // PAIR)]


def moved(value, blocks):
    count = lax.axis_size("dp")
    pairs = [(source, (source + blocks) % count) for source in range(count)]
    return lax.ppermute(value, "dp", pairs)


def split_bf16(value):
    high = value.astype(BF16)
    return high, (value - high.astype(F32)).astype(BF16)


def project_kernel(
    frames_hbm, key_hbm, query_hbm, value_hbm, out_hbm,
    key_ref, value_ref, gram_ref,
    frames_ref, value_weight, out_weight, key_weight, query_weight, rows_ref, sems,
):
    clips, count = gram_ref.shape[0], gram_ref.shape[1]
    scale = frames_ref.shape[1] ** -0.5
    loads = [
        pltpu.make_async_copy(source, held, sems.at[at])
        for at, (source, held) in enumerate((
            (frames_hbm, frames_ref), (value_hbm, value_weight), (out_hbm, out_weight),
            (key_hbm, key_weight), (query_hbm, query_weight),
        ))
    ]
    for load in loads:
        load.start()
    loads[0].wait()
    loads[1].wait()
    rows_ref[...] = jnp.dot(frames_ref[...], value_weight[...], preferred_element_type=F32).astype(BF16)
    loads[2].wait()
    value_ref[...] = jnp.dot(rows_ref[...], out_weight[...], preferred_element_type=F32).astype(BF16)
    loads[3].wait()
    rows_ref[...] = jnp.dot(frames_ref[...], key_weight[...], preferred_element_type=F32).astype(BF16)
    for clip in range(clips):
        own = value_ref[clip * count:(clip + 1) * count, :]
        gram_ref[clip] = lax.dot_general(own, own, ROWS, preferred_element_type=F32)
    loads[4].wait()
    keys = lax.dot_general(rows_ref[...], query_weight[...], ROWS, preferred_element_type=F32)
    key_ref[...] = (keys * scale).astype(BF16)


def score_kernel(
    place_ref, counts_ref, pos_ref, text_ref, key_ref, value_ref, gram_ref,
    similar_ref, loss_ref, terms_ref,
):
    clips, frames = gram_ref.shape[0], gram_ref.shape[1]
    texts = text_ref.shape[0]
    block = texts // (2 * PAIR)
    place = place_ref[0]
    text = text_ref[...]
    scores = lax.dot_general(key_ref[...], text, ROWS, preferred_element_type=F32)
    inner_all = lax.dot_general(value_ref[...], text, ROWS, preferred_element_type=F32)
    text_wide = text.astype(F32)
    sq_high, sq_low = split_bf16(text_wide * text_wide)
    ones = jnp.ones((8, text.shape[1]), BF16)
    text_sq = lax.dot_general(ones, sq_high, ROWS, preferred_element_type=F32)
    text_sq = (text_sq + lax.dot_general(ones, sq_low, ROWS, preferred_element_type=F32))[:1]
    frame_index = lax.broadcasted_iota(jnp.int32, (frames, texts), 0)
    clip_index = lax.broadcasted_iota(jnp.int32, (clips, texts), 0)
    inner = jnp.zeros((clips, texts), F32)
    pooled_sq = jnp.zeros((clips, texts), F32)
    position = jnp.zeros((clips, texts), jnp.int32)
    for clip in range(clips):
        rows = slice(clip * frames, (clip + 1) * frames)
        valid = frame_index < counts_ref[clip]
        score = jnp.where(valid, scores[rows], -jnp.inf)
        weights = jnp.exp(score - jnp.max(score, axis=0, keepdims=True))
        weights = weights * (1.0 / jnp.sum(weights, axis=0, keepdims=True))
        w_high, w_low = split_bf16(weights)
        g_high, g_low = split_bf16(gram_ref[clip])
        mixed = (
            jnp.dot(g_high, w_high, preferred_element_type=F32)
            + jnp.dot(g_high, w_low, preferred_element_type=F32)
            + jnp.dot(g_low, w_high, preferred_element_type=F32)
        )
        here = clip_index == clip
        inner = jnp.where(here, jnp.sum(weights * inner_all[rows], axis=0, keepdims=True), inner)
        pooled_sq = jnp.where(here, jnp.sum(weights * mixed, axis=0, keepdims=True), pooled_sq)
        position = jnp.where(here, pos_ref[clip], position)
    pooled_sq = jnp.maximum(pooled_sq, 0.0)
    similar = LOGIT_SCALE * inner / jnp.sqrt((pooled_sq + EPSILON) * (text_sq + EPSILON))
    lane = lax.broadcasted_iota(jnp.int32, (clips, texts), 1)
    older = lane // SLICE % 2
    hop = place - lane // (2 * block) + 2 * older
    in_block = lane // (2 * SLICE) * SLICE % block + lane % SLICE
    exp_sims = jnp.where((hop >= 0) & (hop <= HOPS), jnp.exp(similar), 0.0)
    terms_ref[...] = jnp.sum(exp_sims, axis=0, keepdims=True)
    similar_ref[...] = similar
    hit = (hop >= 0) & (hop <= HOPS) & (hop * block + in_block == position)
    picked = jnp.sum(jnp.where(hit, similar, 0.0), axis=1, keepdims=True)
    total = jnp.sum(exp_sims, axis=1, keepdims=True)
    loss_ref[...] = jnp.broadcast_to(jnp.log(total) - picked, loss_ref.shape)


def local(frames, texts, w_query, w_key, w_value, w_out, frame_counts, clip_pos):
    clips, frame_total, width = frames.shape
    slice_rows = texts.shape[0]
    tm_count = lax.axis_size("tm")
    groups = pair_groups(lax.axis_size("dp"), tm_count)
    peers = PAIR * tm_count
    block_rows = slice_rows * tm_count
    place = lax.axis_index("dp") % PAIR

    outgoing = lax.optimization_barrier(jnp.broadcast_to(texts[None, None], (peers, 2, slice_rows, width)))
    before = jnp.broadcast_to(moved(texts, 2)[None, None], (peers, 1, slice_rows, width))
    outgoing = lax.dynamic_update_slice(outgoing, before, (0, 1, 0, 0))
    band_text = lax.all_to_all(
        outgoing.reshape(peers, 2 * slice_rows, width),
        BOTH, 0, 0, axis_index_groups=groups, tiled=True,
    ).reshape(2 * peers * slice_rows, width)

    smem = pl.BlockSpec(memory_space=pltpu.SMEM)
    vmem = pl.BlockSpec(memory_space=pltpu.VMEM)
    rows = clips * frame_total
    key_rows, value_rows, gram = pl.pallas_call(
        project_kernel,
        in_specs=[pl.BlockSpec(memory_space=pltpu.HBM)] * 5,
        out_specs=[vmem] * 3,
        out_shape=[
            jax.ShapeDtypeStruct((rows, width), BF16),
            jax.ShapeDtypeStruct((rows, width), BF16),
            jax.ShapeDtypeStruct((clips, frame_total, frame_total), F32),
        ],
        scratch_shapes=[
            pltpu.VMEM((rows, width), BF16),
            *[pltpu.VMEM((width, width), BF16)] * 4,
            pltpu.VMEM((rows, width), BF16),
            pltpu.SemaphoreType.DMA((5,)),
        ],
        compiler_params=pltpu.CompilerParams(vmem_limit_bytes=52 * 1024 * 1024),
        cost_estimate=pl.CostEstimate(
            flops=8 * rows * width * width, bytes_accessed=8 * width * width, transcendentals=0
        ),
    )(frames.reshape(rows, width), w_key, w_query, w_value, w_out)

    similar, loss, terms = pl.pallas_call(
        score_kernel,
        in_specs=[smem] * 3 + [vmem] * 4,
        out_specs=[vmem] * 3,
        out_shape=[
            jax.ShapeDtypeStruct((clips, 2 * peers * slice_rows), F32),
            jax.ShapeDtypeStruct((clips, 128), F32),
            jax.ShapeDtypeStruct((1, 2 * peers * slice_rows), F32),
        ],
        compiler_params=pltpu.CompilerParams(vmem_limit_bytes=24 * 1024 * 1024),
        cost_estimate=pl.CostEstimate(flops=500_000_000, bytes_accessed=3_000_000, transcendentals=120_000),
    )(place.reshape(1), frame_counts, clip_pos, band_text, key_rows, value_rows, gram)

    similar, loss, terms = lax.optimization_barrier((similar, loss, terms))
    met = jnp.broadcast_to(terms[None], (peers,) + terms.shape)
    met = lax.all_to_all(met, BOTH, 0, 0, axis_index_groups=groups, tiled=True)
    home = (place * tm_count + lax.axis_index("tm")) * 2 * slice_rows
    met = lax.dynamic_slice_in_dim(jnp.sum(met, axis=(0, 1)), home, 2 * slice_rows)
    text_lse = jnp.log(met[:slice_rows] + moved(met[slice_rows:], -2))

    similar = similar.reshape(clips, PAIR, tm_count, 2, slice_rows)

    def part(which, older):
        return similar[:, which, :, older, :].reshape(clips, block_rows)

    first = place == 0
    by_hop = [
        jnp.where(first, part(0, 0), part(1, 0)),
        jnp.where(first, part(1, 1), part(0, 0)),
        jnp.where(first, part(0, 1), part(1, 1)),
    ]
    return (jnp.stack(by_hop, axis=1), loss[:, 0], text_lse)


def solution(mesh):
    in_specs = (
        P(BOTH, None, None), P(BOTH, None), P(), P(), P(), P(), P(BOTH), P(BOTH),
    )
    out_specs = (P(BOTH, None, None), P(BOTH), P(BOTH))
    return jax.shard_map(local, mesh=mesh, in_specs=in_specs, out_specs=out_specs, check_vma=False)
```

```python
import jax
import jax.numpy as jnp
from jax import lax
from jax.experimental import pallas as pl
from jax.experimental.pallas import tpu as pltpu
from jax.sharding import PartitionSpec as P

HOPS = 2
RING = 4
PAIR = 2
LOGIT_SCALE = 32.0
EPSILON = 1e-06
SLICE = 8
BOTH = ("dp", "tm")
F32 = jnp.float32
BF16 = jnp.bfloat16
ROWS = (((1,), (1,)), ((), ()))


def block_groups(dp_count, tm_count, blocks):
    width = blocks * tm_count
    return [list(range(g * width, (g + 1) * width)) for g in range(dp_count // blocks)]


def moved(value, blocks, places=range(RING)):
    count = lax.axis_size("dp")
    pairs = [(source, (source + blocks) % count) for source in range(count) if source % RING in places]
    return lax.ppermute(value, "dp", pairs)


def split_bf16(value):
    high = value.astype(BF16)
    return high, (value - high.astype(F32)).astype(BF16)


def project_kernel(
    frames_hbm, key_hbm, query_hbm, value_hbm, out_hbm,
    key_ref, value_ref, gram_ref,
    frames_ref, value_weight, out_weight, key_weight, query_weight, rows_ref, sems,
):
    clips, count = gram_ref.shape[0], gram_ref.shape[1]
    scale = frames_ref.shape[1] ** -0.5
    loads = [
        pltpu.make_async_copy(source, held, sems.at[at])
        for at, (source, held) in enumerate((
            (frames_hbm, frames_ref), (value_hbm, value_weight), (out_hbm, out_weight),
            (key_hbm, key_weight), (query_hbm, query_weight),
        ))
    ]
    for load in loads:
        load.start()
    loads[0].wait()
    loads[1].wait()
    rows_ref[...] = jnp.dot(frames_ref[...], value_weight[...], preferred_element_type=F32).astype(BF16)
    loads[2].wait()
    value_ref[...] = jnp.dot(rows_ref[...], out_weight[...], preferred_element_type=F32).astype(BF16)
    loads[3].wait()
    rows_ref[...] = jnp.dot(frames_ref[...], key_weight[...], preferred_element_type=F32).astype(BF16)
    for clip in range(clips):
        own = value_ref[clip * count:(clip + 1) * count, :]
        gram_ref[clip] = lax.dot_general(own, own, ROWS, preferred_element_type=F32)
    loads[4].wait()
    keys = lax.dot_general(rows_ref[...], query_weight[...], ROWS, preferred_element_type=F32)
    key_ref[...] = (keys * scale).astype(BF16)


def score_kernel(
    place_ref, counts_ref, pos_ref, text_ref, key_ref, value_ref, gram_ref,
    similar_ref, loss_ref, terms_ref,
):
    clips, frames = gram_ref.shape[0], gram_ref.shape[1]
    texts = text_ref.shape[0]
    block = texts // (2 * PAIR)
    place = place_ref[0]
    text = text_ref[...]
    scores = lax.dot_general(key_ref[...], text, ROWS, preferred_element_type=F32)
    inner_all = lax.dot_general(value_ref[...], text, ROWS, preferred_element_type=F32)
    text_wide = text.astype(F32)
    sq_high, sq_low = split_bf16(text_wide * text_wide)
    ones = jnp.ones((8, text.shape[1]), BF16)
    text_sq = lax.dot_general(ones, sq_high, ROWS, preferred_element_type=F32)
    text_sq = (text_sq + lax.dot_general(ones, sq_low, ROWS, preferred_element_type=F32))[:1]
    frame_index = lax.broadcasted_iota(jnp.int32, (frames, texts), 0)
    clip_index = lax.broadcasted_iota(jnp.int32, (clips, texts), 0)
    inner = jnp.zeros((clips, texts), F32)
    pooled_sq = jnp.zeros((clips, texts), F32)
    position = jnp.zeros((clips, texts), jnp.int32)
    for clip in range(clips):
        rows = slice(clip * frames, (clip + 1) * frames)
        valid = frame_index < counts_ref[clip]
        score = jnp.where(valid, scores[rows], -jnp.inf)
        weights = jnp.exp(score - jnp.max(score, axis=0, keepdims=True))
        weights = weights * (1.0 / jnp.sum(weights, axis=0, keepdims=True))
        w_high, w_low = split_bf16(weights)
        g_high, g_low = split_bf16(gram_ref[clip])
        mixed = (
            jnp.dot(g_high, w_high, preferred_element_type=F32)
            + jnp.dot(g_high, w_low, preferred_element_type=F32)
            + jnp.dot(g_low, w_high, preferred_element_type=F32)
        )
        here = clip_index == clip
        inner = jnp.where(here, jnp.sum(weights * inner_all[rows], axis=0, keepdims=True), inner)
        pooled_sq = jnp.where(here, jnp.sum(weights * mixed, axis=0, keepdims=True), pooled_sq)
        position = jnp.where(here, pos_ref[clip], position)
    pooled_sq = jnp.maximum(pooled_sq, 0.0)
    similar = LOGIT_SCALE * inner / jnp.sqrt((pooled_sq + EPSILON) * (text_sq + EPSILON))
    lane = lax.broadcasted_iota(jnp.int32, (clips, texts), 1)
    older = lane // SLICE % 2
    hop = place - lane // (2 * block) + 2 * older
    in_block = lane // (2 * SLICE) * SLICE % block + lane % SLICE
    exp_sims = jnp.where((hop >= 0) & (hop <= HOPS), jnp.exp(similar), 0.0)
    terms_ref[...] = jnp.sum(exp_sims, axis=0, keepdims=True)
    similar_ref[...] = similar
    hit = (hop >= 0) & (hop <= HOPS) & (hop * block + in_block == position)
    picked = jnp.sum(jnp.where(hit, similar, 0.0), axis=1, keepdims=True)
    total = jnp.sum(exp_sims, axis=1, keepdims=True)
    loss_ref[...] = jnp.broadcast_to(jnp.log(total) - picked, loss_ref.shape)


def local(frames, texts, w_query, w_key, w_value, w_out, frame_counts, clip_pos):
    clips, frame_total, width = frames.shape
    slice_rows = texts.shape[0]
    tm_count = lax.axis_size("tm")
    dp_count = lax.axis_size("dp")
    groups = block_groups(dp_count, tm_count, PAIR)
    peers = PAIR * tm_count
    block_rows = slice_rows * tm_count
    place = lax.axis_index("dp") % PAIR

    outgoing = lax.optimization_barrier(jnp.broadcast_to(texts[None, None], (peers, 2, slice_rows, width)))
    before = jnp.broadcast_to(moved(texts, 2)[None, None], (peers, 1, slice_rows, width))
    outgoing = lax.dynamic_update_slice(outgoing, before, (0, 1, 0, 0))
    band_text = lax.all_to_all(
        outgoing.reshape(peers, 2 * slice_rows, width),
        BOTH, 0, 0, axis_index_groups=groups, tiled=True,
    ).reshape(2 * peers * slice_rows, width)

    smem = pl.BlockSpec(memory_space=pltpu.SMEM)
    vmem = pl.BlockSpec(memory_space=pltpu.VMEM)
    rows = clips * frame_total
    key_rows, value_rows, gram = pl.pallas_call(
        project_kernel,
        in_specs=[pl.BlockSpec(memory_space=pltpu.HBM)] * 5,
        out_specs=[vmem] * 3,
        out_shape=[
            jax.ShapeDtypeStruct((rows, width), BF16),
            jax.ShapeDtypeStruct((rows, width), BF16),
            jax.ShapeDtypeStruct((clips, frame_total, frame_total), F32),
        ],
        scratch_shapes=[
            pltpu.VMEM((rows, width), BF16),
            *[pltpu.VMEM((width, width), BF16)] * 4,
            pltpu.VMEM((rows, width), BF16),
            pltpu.SemaphoreType.DMA((5,)),
        ],
        compiler_params=pltpu.CompilerParams(vmem_limit_bytes=52 * 1024 * 1024),
        cost_estimate=pl.CostEstimate(
            flops=8 * rows * width * width, bytes_accessed=8 * width * width, transcendentals=0
        ),
    )(frames.reshape(rows, width), w_key, w_query, w_value, w_out)

    similar, loss, terms = pl.pallas_call(
        score_kernel,
        in_specs=[smem] * 3 + [vmem] * 4,
        out_specs=[vmem] * 3,
        out_shape=[
            jax.ShapeDtypeStruct((clips, 2 * peers * slice_rows), F32),
            jax.ShapeDtypeStruct((clips, 128), F32),
            jax.ShapeDtypeStruct((1, 2 * peers * slice_rows), F32),
        ],
        compiler_params=pltpu.CompilerParams(vmem_limit_bytes=24 * 1024 * 1024),
        cost_estimate=pl.CostEstimate(flops=500_000_000, bytes_accessed=3_000_000, transcendentals=120_000),
    )(place.reshape(1), frame_counts, clip_pos, band_text, key_rows, value_rows, gram)

    similar, loss, terms = lax.optimization_barrier((similar, loss, terms))
    met = jnp.broadcast_to(terms[None], (RING * tm_count,) + terms.shape)
    met = lax.all_to_all(
        met, BOTH, 0, 0, axis_index_groups=block_groups(dp_count, tm_count, RING), tiled=True
    )
    met = jnp.sum(met.reshape(RING // PAIR, peers, -1), axis=1)
    home = (place * tm_count + lax.axis_index("tm")) * 2 * slice_rows
    met = lax.dynamic_slice_in_dim(met, home, 2 * slice_rows, axis=1)
    later = lax.axis_index("dp") % RING >= PAIR
    newer = jnp.where(later, met[1, :slice_rows], met[0, :slice_rows])
    older = jnp.where(later, met[0, slice_rows:], met[1, slice_rows:])
    beyond = moved(older, -RING, range(PAIR, RING))
    text_lse = jnp.log(newer + jnp.where(later, beyond, older))

    similar = similar.reshape(clips, PAIR, tm_count, 2, slice_rows)

    def part(which, older):
        return similar[:, which, :, older, :].reshape(clips, block_rows)

    first = place == 0
    by_hop = [
        jnp.where(first, part(0, 0), part(1, 0)),
        jnp.where(first, part(1, 1), part(0, 0)),
        jnp.where(first, part(0, 1), part(1, 1)),
    ]
    return (jnp.stack(by_hop, axis=1), loss[:, 0], text_lse)


def solution(mesh):
    in_specs = (
        P(BOTH, None, None), P(BOTH, None), P(), P(), P(), P(), P(BOTH), P(BOTH),
    )
    out_specs = (P(BOTH, None, None), P(BOTH), P(BOTH))
    return jax.shard_map(local, mesh=mesh, in_specs=in_specs, out_specs=out_specs, check_vma=False)
```

```python
import jax
import jax.numpy as jnp
from jax import lax
from jax.experimental import pallas as pl
from jax.experimental.pallas import tpu as pltpu
from jax.sharding import PartitionSpec as P

HOPS = 2
RING = 4
PAIR = 2
LOGIT_SCALE = 32.0
EPSILON = 1e-06
SLICE = 8
BOTH = ("dp", "tm")
F32 = jnp.float32
BF16 = jnp.bfloat16
ROWS = (((1,), (1,)), ((), ()))


def block_groups(dp_count, tm_count, blocks):
    width = blocks * tm_count
    return [list(range(g * width, (g + 1) * width)) for g in range(dp_count // blocks)]


def moved(value, blocks, places=range(RING)):
    count = lax.axis_size("dp")
    pairs = [(source, (source + blocks) % count) for source in range(count) if source % RING in places]
    return lax.ppermute(value, "dp", pairs)


def split_bf16(value):
    high = value.astype(BF16)
    return high, (value - high.astype(F32)).astype(BF16)


def project_kernel(
    frames_hbm, key_hbm, query_hbm, value_hbm, out_hbm,
    key_ref, value_ref, gram_ref,
    frames_ref, value_weight, out_weight, key_weight, query_weight, rows_ref, sems,
):
    clips, count = gram_ref.shape[0], gram_ref.shape[1]
    scale = frames_ref.shape[1] ** -0.5
    loads = [
        pltpu.make_async_copy(source, held, sems.at[at])
        for at, (source, held) in enumerate((
            (frames_hbm, frames_ref), (value_hbm, value_weight), (out_hbm, out_weight),
            (key_hbm, key_weight), (query_hbm, query_weight),
        ))
    ]
    for load in loads:
        load.start()
    loads[0].wait()
    loads[1].wait()
    rows_ref[...] = jnp.dot(frames_ref[...], value_weight[...], preferred_element_type=F32).astype(BF16)
    loads[2].wait()
    value_ref[...] = jnp.dot(rows_ref[...], out_weight[...], preferred_element_type=F32).astype(BF16)
    loads[3].wait()
    rows_ref[...] = jnp.dot(frames_ref[...], key_weight[...], preferred_element_type=F32).astype(BF16)
    for clip in range(clips):
        own = value_ref[clip * count:(clip + 1) * count, :]
        gram_ref[clip] = lax.dot_general(own, own, ROWS, preferred_element_type=F32)
    loads[4].wait()
    keys = lax.dot_general(rows_ref[...], query_weight[...], ROWS, preferred_element_type=F32)
    key_ref[...] = (keys * scale).astype(BF16)


def score_kernel(
    place_ref, counts_ref, pos_ref, text_ref, key_ref, value_ref, gram_ref,
    similar_ref, loss_ref, terms_ref,
):
    clips, frames = gram_ref.shape[0], gram_ref.shape[1]
    texts = text_ref.shape[0]
    block = texts // (2 * PAIR)
    place = place_ref[0]
    text = text_ref[...]
    scores = lax.dot_general(key_ref[...], text, ROWS, preferred_element_type=F32)
    inner_all = lax.dot_general(value_ref[...], text, ROWS, preferred_element_type=F32)
    text_wide = text.astype(F32)
    sq_high, sq_low = split_bf16(text_wide * text_wide)
    ones = jnp.ones((8, text.shape[1]), BF16)
    text_sq = lax.dot_general(ones, sq_high, ROWS, preferred_element_type=F32)
    text_sq = (text_sq + lax.dot_general(ones, sq_low, ROWS, preferred_element_type=F32))[:1]
    frame_index = lax.broadcasted_iota(jnp.int32, (frames, texts), 0)
    clip_index = lax.broadcasted_iota(jnp.int32, (clips, texts), 0)
    inner = jnp.zeros((clips, texts), F32)
    pooled_sq = jnp.zeros((clips, texts), F32)
    position = jnp.zeros((clips, texts), jnp.int32)
    for clip in range(clips):
        rows = slice(clip * frames, (clip + 1) * frames)
        valid = frame_index < counts_ref[clip]
        score = jnp.where(valid, scores[rows], -jnp.inf)
        weights = jnp.exp(score - jnp.max(score, axis=0, keepdims=True))
        weights = weights * (1.0 / jnp.sum(weights, axis=0, keepdims=True))
        w_high, w_low = split_bf16(weights)
        g_high, g_low = split_bf16(gram_ref[clip])
        mixed = (
            jnp.dot(g_high, w_high, preferred_element_type=F32)
            + jnp.dot(g_high, w_low, preferred_element_type=F32)
            + jnp.dot(g_low, w_high, preferred_element_type=F32)
        )
        here = clip_index == clip
        inner = jnp.where(here, jnp.sum(weights * inner_all[rows], axis=0, keepdims=True), inner)
        pooled_sq = jnp.where(here, jnp.sum(weights * mixed, axis=0, keepdims=True), pooled_sq)
        position = jnp.where(here, pos_ref[clip], position)
    pooled_sq = jnp.maximum(pooled_sq, 0.0)
    similar = LOGIT_SCALE * inner / jnp.sqrt((pooled_sq + EPSILON) * (text_sq + EPSILON))
    lane = lax.broadcasted_iota(jnp.int32, (clips, texts), 1)
    older = lane // SLICE % 2
    bringer = lane // (2 * block)
    hop = place + jnp.where(older == 1, bringer + 1, -bringer)
    in_block = lane // (2 * SLICE) * SLICE % block + lane % SLICE
    exp_sims = jnp.where((hop >= 0) & (hop <= HOPS), jnp.exp(similar), 0.0)
    terms_ref[...] = jnp.sum(exp_sims, axis=0, keepdims=True)
    similar_ref[...] = similar
    hit = (hop >= 0) & (hop <= HOPS) & (hop * block + in_block == position)
    picked = jnp.sum(jnp.where(hit, similar, 0.0), axis=1, keepdims=True)
    total = jnp.sum(exp_sims, axis=1, keepdims=True)
    loss_ref[...] = jnp.broadcast_to(jnp.log(total) - picked, loss_ref.shape)


def local(frames, texts, w_query, w_key, w_value, w_out, frame_counts, clip_pos):
    clips, frame_total, width = frames.shape
    slice_rows = texts.shape[0]
    tm_count = lax.axis_size("tm")
    dp_count = lax.axis_size("dp")
    groups = block_groups(dp_count, tm_count, PAIR)
    peers = PAIR * tm_count
    block_rows = slice_rows * tm_count
    place = lax.axis_index("dp") % PAIR

    outgoing = lax.optimization_barrier(jnp.broadcast_to(texts[None, None], (peers, 2, slice_rows, width)))
    crossed = [(source, (source + (1 if source % PAIR else 3)) % dp_count) for source in range(dp_count)]
    before = lax.ppermute(texts, "dp", crossed)
    before = jnp.broadcast_to(before[None, None], (peers, 1, slice_rows, width))
    outgoing = lax.dynamic_update_slice(outgoing, before, (0, 1, 0, 0))
    band_text = lax.all_to_all(
        outgoing.reshape(peers, 2 * slice_rows, width),
        BOTH, 0, 0, axis_index_groups=groups, tiled=True,
    ).reshape(2 * peers * slice_rows, width)

    smem = pl.BlockSpec(memory_space=pltpu.SMEM)
    vmem = pl.BlockSpec(memory_space=pltpu.VMEM)
    rows = clips * frame_total
    key_rows, value_rows, gram = pl.pallas_call(
        project_kernel,
        in_specs=[pl.BlockSpec(memory_space=pltpu.HBM)] * 5,
        out_specs=[vmem] * 3,
        out_shape=[
            jax.ShapeDtypeStruct((rows, width), BF16),
            jax.ShapeDtypeStruct((rows, width), BF16),
            jax.ShapeDtypeStruct((clips, frame_total, frame_total), F32),
        ],
        scratch_shapes=[
            pltpu.VMEM((rows, width), BF16),
            *[pltpu.VMEM((width, width), BF16)] * 4,
            pltpu.VMEM((rows, width), BF16),
            pltpu.SemaphoreType.DMA((5,)),
        ],
        compiler_params=pltpu.CompilerParams(vmem_limit_bytes=52 * 1024 * 1024),
        cost_estimate=pl.CostEstimate(
            flops=8 * rows * width * width, bytes_accessed=8 * width * width, transcendentals=0
        ),
    )(frames.reshape(rows, width), w_key, w_query, w_value, w_out)

    similar, loss, terms = pl.pallas_call(
        score_kernel,
        in_specs=[smem] * 3 + [vmem] * 4,
        out_specs=[vmem] * 3,
        out_shape=[
            jax.ShapeDtypeStruct((clips, 2 * peers * slice_rows), F32),
            jax.ShapeDtypeStruct((clips, 128), F32),
            jax.ShapeDtypeStruct((1, 2 * peers * slice_rows), F32),
        ],
        compiler_params=pltpu.CompilerParams(vmem_limit_bytes=24 * 1024 * 1024),
        cost_estimate=pl.CostEstimate(flops=500_000_000, bytes_accessed=3_000_000, transcendentals=120_000),
    )(place.reshape(1), frame_counts, clip_pos, band_text, key_rows, value_rows, gram)

    similar, loss, terms = lax.optimization_barrier((similar, loss, terms))
    met = jnp.broadcast_to(terms[None], (RING * tm_count,) + terms.shape)
    met = lax.all_to_all(
        met, BOTH, 0, 0, axis_index_groups=block_groups(dp_count, tm_count, RING), tiled=True
    )
    met = jnp.sum(met.reshape(RING // PAIR, peers, -1), axis=1)
    mine = lax.axis_index("tm") * 2 * slice_rows
    half = 2 * block_rows
    newer = lax.dynamic_slice_in_dim(met, place * half + mine, slice_rows, axis=1)
    older = lax.dynamic_slice_in_dim(met, (1 - place) * half + mine + slice_rows, slice_rows, axis=1)
    later = lax.axis_index("dp") % RING >= PAIR
    newer = jnp.where(later, newer[1], newer[0])
    older = jnp.where(later, older[0], older[1])
    beyond = moved(older, -RING, range(PAIR, RING))
    text_lse = jnp.log(newer + jnp.where(later, beyond, older))

    similar = similar.reshape(clips, PAIR, tm_count, 2, slice_rows)

    def part(which, older):
        return similar[:, which, :, older, :].reshape(clips, block_rows)

    first = place == 0
    by_hop = [
        jnp.where(first, part(0, 0), part(1, 0)),
        jnp.where(first, part(0, 1), part(0, 0)),
        jnp.where(first, part(1, 1), part(0, 1)),
    ]
    return (jnp.stack(by_hop, axis=1), loss[:, 0], text_lse)


def solution(mesh):
    in_specs = (
        P(BOTH, None, None), P(BOTH, None), P(), P(), P(), P(), P(BOTH), P(BOTH),
    )
    out_specs = (P(BOTH, None, None), P(BOTH), P(BOTH))
    return jax.shard_map(local, mesh=mesh, in_specs=in_specs, out_specs=out_specs, check_vma=False)
```

```python
import jax
import jax.numpy as jnp
from jax import lax
from jax.experimental import pallas as pl
from jax.experimental.pallas import tpu as pltpu
from jax.sharding import PartitionSpec as P

HOPS = 2
RING = 4
PAIR = 2
LOGIT_SCALE = 32.0
EPSILON = 1e-06
SLICE = 8
BOTH = ("dp", "tm")
F32 = jnp.float32
BF16 = jnp.bfloat16
ROWS = (((1,), (1,)), ((), ()))


def block_groups(dp_count, tm_count, blocks):
    width = blocks * tm_count
    return [list(range(g * width, (g + 1) * width)) for g in range(dp_count // blocks)]


def moved(value, blocks, places=range(RING)):
    count = lax.axis_size("dp")
    pairs = [(source, (source + blocks) % count) for source in range(count) if source % RING in places]
    return lax.ppermute(value, "dp", pairs)


def split_bf16(value):
    high = value.astype(BF16)
    return high, (value - high.astype(F32)).astype(BF16)


def project_kernel(
    frames_hbm, key_hbm, query_hbm, value_hbm, out_hbm,
    key_ref, value_ref, gram_ref,
    frames_ref, value_weight, out_weight, key_weight, query_weight, rows_ref, sems,
):
    clips, count = gram_ref.shape[0], gram_ref.shape[1]
    scale = frames_ref.shape[1] ** -0.5
    loads = [
        pltpu.make_async_copy(source, held, sems.at[at])
        for at, (source, held) in enumerate((
            (frames_hbm, frames_ref), (value_hbm, value_weight), (out_hbm, out_weight),
            (key_hbm, key_weight), (query_hbm, query_weight),
        ))
    ]
    for load in loads:
        load.start()
    loads[0].wait()
    loads[1].wait()
    rows_ref[...] = jnp.dot(frames_ref[...], value_weight[...], preferred_element_type=F32).astype(BF16)
    loads[2].wait()
    value_ref[...] = jnp.dot(rows_ref[...], out_weight[...], preferred_element_type=F32).astype(BF16)
    loads[3].wait()
    rows_ref[...] = jnp.dot(frames_ref[...], key_weight[...], preferred_element_type=F32).astype(BF16)
    for clip in range(clips):
        own = value_ref[clip * count:(clip + 1) * count, :]
        gram_ref[clip] = lax.dot_general(own, own, ROWS, preferred_element_type=F32)
    loads[4].wait()
    keys = lax.dot_general(rows_ref[...], query_weight[...], ROWS, preferred_element_type=F32)
    key_ref[...] = (keys * scale).astype(BF16)


def score_kernel(
    place_ref, counts_ref, pos_ref, text_ref, key_ref, value_ref, gram_ref,
    similar_ref, loss_ref, terms_ref,
):
    clips, frames = gram_ref.shape[0], gram_ref.shape[1]
    texts = text_ref.shape[0]
    block = texts // (2 * PAIR)
    place = place_ref[0]
    text = text_ref[...]
    scores = lax.dot_general(key_ref[...], text, ROWS, preferred_element_type=F32)
    inner_all = lax.dot_general(value_ref[...], text, ROWS, preferred_element_type=F32)
    text_wide = text.astype(F32)
    sq_high, sq_low = split_bf16(text_wide * text_wide)
    ones = jnp.ones((8, text.shape[1]), BF16)
    text_sq = lax.dot_general(ones, sq_high, ROWS, preferred_element_type=F32)
    text_sq = (text_sq + lax.dot_general(ones, sq_low, ROWS, preferred_element_type=F32))[:1]
    frame_index = lax.broadcasted_iota(jnp.int32, (frames, texts), 0)
    clip_index = lax.broadcasted_iota(jnp.int32, (clips, texts), 0)
    inner = jnp.zeros((clips, texts), F32)
    pooled_sq = jnp.zeros((clips, texts), F32)
    position = jnp.zeros((clips, texts), jnp.int32)
    for clip in range(clips):
        rows = slice(clip * frames, (clip + 1) * frames)
        valid = frame_index < counts_ref[clip]
        score = jnp.where(valid, scores[rows], -jnp.inf)
        weights = jnp.exp(score - jnp.max(score, axis=0, keepdims=True))
        weights = weights * (1.0 / jnp.sum(weights, axis=0, keepdims=True))
        w_high, w_low = split_bf16(weights)
        g_high, g_low = split_bf16(gram_ref[clip])
        mixed = (
            jnp.dot(g_high, w_high, preferred_element_type=F32)
            + jnp.dot(g_high, w_low, preferred_element_type=F32)
            + jnp.dot(g_low, w_high, preferred_element_type=F32)
        )
        here = clip_index == clip
        inner = jnp.where(here, jnp.sum(weights * inner_all[rows], axis=0, keepdims=True), inner)
        pooled_sq = jnp.where(here, jnp.sum(weights * mixed, axis=0, keepdims=True), pooled_sq)
        position = jnp.where(here, pos_ref[clip], position)
    pooled_sq = jnp.maximum(pooled_sq, 0.0)
    similar = LOGIT_SCALE * inner / jnp.sqrt((pooled_sq + EPSILON) * (text_sq + EPSILON))
    lane = lax.broadcasted_iota(jnp.int32, (clips, texts), 1)
    older = lane // SLICE % 2
    bringer = lane // (2 * block)
    hop = place + jnp.where(older == 1, bringer + 1, -bringer)
    in_block = lane // (2 * SLICE) * SLICE % block + lane % SLICE
    exp_sims = jnp.where((hop >= 0) & (hop <= HOPS), jnp.exp(similar), 0.0)
    terms_ref[...] = jnp.broadcast_to(jnp.sum(exp_sims, axis=0, keepdims=True)[None], terms_ref.shape)
    similar_ref[...] = similar
    hit = (hop >= 0) & (hop <= HOPS) & (hop * block + in_block == position)
    picked = jnp.sum(jnp.where(hit, similar, 0.0), axis=1, keepdims=True)
    total = jnp.sum(exp_sims, axis=1, keepdims=True)
    loss_ref[...] = jnp.broadcast_to(jnp.log(total) - picked, loss_ref.shape)


def local(frames, texts, w_query, w_key, w_value, w_out, frame_counts, clip_pos):
    clips, frame_total, width = frames.shape
    slice_rows = texts.shape[0]
    tm_count = lax.axis_size("tm")
    dp_count = lax.axis_size("dp")
    groups = block_groups(dp_count, tm_count, PAIR)
    peers = PAIR * tm_count
    block_rows = slice_rows * tm_count
    place = lax.axis_index("dp") % PAIR

    outgoing = lax.optimization_barrier(jnp.broadcast_to(texts[None, None], (peers, 2, slice_rows, width)))
    crossed = [(source, (source + (1 if source % PAIR else 3)) % dp_count) for source in range(dp_count)]
    before = lax.ppermute(texts, "dp", crossed)
    before = jnp.broadcast_to(before[None, None], (peers, 1, slice_rows, width))
    outgoing = lax.dynamic_update_slice(outgoing, before, (0, 1, 0, 0))
    band_text = lax.all_to_all(
        outgoing.reshape(peers, 2 * slice_rows, width),
        BOTH, 0, 0, axis_index_groups=groups, tiled=True,
    ).reshape(2 * peers * slice_rows, width)

    smem = pl.BlockSpec(memory_space=pltpu.SMEM)
    vmem = pl.BlockSpec(memory_space=pltpu.VMEM)
    rows = clips * frame_total
    key_rows, value_rows, gram = pl.pallas_call(
        project_kernel,
        in_specs=[pl.BlockSpec(memory_space=pltpu.HBM)] * 5,
        out_specs=[vmem] * 3,
        out_shape=[
            jax.ShapeDtypeStruct((rows, width), BF16),
            jax.ShapeDtypeStruct((rows, width), BF16),
            jax.ShapeDtypeStruct((clips, frame_total, frame_total), F32),
        ],
        scratch_shapes=[
            pltpu.VMEM((rows, width), BF16),
            *[pltpu.VMEM((width, width), BF16)] * 4,
            pltpu.VMEM((rows, width), BF16),
            pltpu.SemaphoreType.DMA((5,)),
        ],
        compiler_params=pltpu.CompilerParams(vmem_limit_bytes=52 * 1024 * 1024),
        cost_estimate=pl.CostEstimate(
            flops=8 * rows * width * width, bytes_accessed=8 * width * width, transcendentals=0
        ),
    )(frames.reshape(rows, width), w_key, w_query, w_value, w_out)

    similar, loss, terms = pl.pallas_call(
        score_kernel,
        in_specs=[smem] * 3 + [vmem] * 4,
        out_specs=[vmem] * 3,
        out_shape=[
            jax.ShapeDtypeStruct((clips, 2 * peers * slice_rows), F32),
            jax.ShapeDtypeStruct((clips, 128), F32),
            jax.ShapeDtypeStruct((RING * tm_count, 1, 2 * peers * slice_rows), F32),
        ],
        compiler_params=pltpu.CompilerParams(vmem_limit_bytes=24 * 1024 * 1024),
        cost_estimate=pl.CostEstimate(flops=500_000_000, bytes_accessed=3_000_000, transcendentals=120_000),
    )(place.reshape(1), frame_counts, clip_pos, band_text, key_rows, value_rows, gram)

    similar, loss, terms = lax.optimization_barrier((similar, loss, terms))
    met = lax.all_to_all(
        terms, BOTH, 0, 0, axis_index_groups=block_groups(dp_count, tm_count, RING), tiled=True
    )
    met = jnp.sum(met.reshape(RING // PAIR, peers, -1), axis=1)
    mine = lax.axis_index("tm") * 2 * slice_rows
    half = 2 * block_rows
    newer = lax.dynamic_slice_in_dim(met, place * half + mine, slice_rows, axis=1)
    older = lax.dynamic_slice_in_dim(met, (1 - place) * half + mine + slice_rows, slice_rows, axis=1)
    later = lax.axis_index("dp") % RING >= PAIR
    newer = jnp.where(later, newer[1], newer[0])
    older = jnp.where(later, older[0], older[1])
    beyond = moved(older, -RING, range(PAIR, RING))
    text_lse = jnp.log(newer + jnp.where(later, beyond, older))

    similar = similar.reshape(clips, PAIR, tm_count, 2, slice_rows)

    def part(which, older):
        return similar[:, which, :, older, :].reshape(clips, block_rows)

    first = place == 0
    by_hop = [
        jnp.where(first, part(0, 0), part(1, 0)),
        jnp.where(first, part(0, 1), part(0, 0)),
        jnp.where(first, part(1, 1), part(0, 1)),
    ]
    return (jnp.stack(by_hop, axis=1), loss[:, 0], text_lse)


def solution(mesh):
    in_specs = (
        P(BOTH, None, None), P(BOTH, None), P(), P(), P(), P(), P(BOTH), P(BOTH),
    )
    out_specs = (P(BOTH, None, None), P(BOTH), P(BOTH))
    return jax.shard_map(local, mesh=mesh, in_specs=in_specs, out_specs=out_specs, check_vma=False)
```

```python
import jax
import jax.numpy as jnp
from jax import lax
from jax.experimental import pallas as pl
from jax.experimental.pallas import tpu as pltpu
from jax.sharding import PartitionSpec as P

HOPS = 2
RING = 4
PAIR = 2
LOGIT_SCALE = 32.0
EPSILON = 1e-06
SLICE = 8
BOTH = ("dp", "tm")
F32 = jnp.float32
BF16 = jnp.bfloat16
ROWS = (((1,), (1,)), ((), ()))


def block_groups(dp_count, tm_count, blocks):
    width = blocks * tm_count
    return [list(range(g * width, (g + 1) * width)) for g in range(dp_count // blocks)]


def moved(value, blocks, places=range(RING)):
    count = lax.axis_size("dp")
    pairs = [(source, (source + blocks) % count) for source in range(count) if source % RING in places]
    return lax.ppermute(value, "dp", pairs)


def split_bf16(value):
    high = value.astype(BF16)
    return high, (value - high.astype(F32)).astype(BF16)


def project_kernel(
    frames_hbm, key_hbm, query_hbm, value_hbm, out_hbm,
    key_ref, value_ref, gram_ref,
    frames_ref, value_weight, out_weight, key_weight, query_weight, rows_ref, sems,
):
    clips, count = gram_ref.shape[0], gram_ref.shape[1]
    scale = frames_ref.shape[1] ** -0.5
    loads = [
        pltpu.make_async_copy(source, held, sems.at[at])
        for at, (source, held) in enumerate((
            (frames_hbm, frames_ref), (value_hbm, value_weight), (out_hbm, out_weight),
            (key_hbm, key_weight), (query_hbm, query_weight),
        ))
    ]
    for load in loads:
        load.start()
    loads[0].wait()
    loads[1].wait()
    rows_ref[...] = jnp.dot(frames_ref[...], value_weight[...], preferred_element_type=F32).astype(BF16)
    loads[2].wait()
    value_ref[...] = jnp.dot(rows_ref[...], out_weight[...], preferred_element_type=F32).astype(BF16)
    loads[3].wait()
    rows_ref[...] = jnp.dot(frames_ref[...], key_weight[...], preferred_element_type=F32).astype(BF16)
    for clip in range(clips):
        own = value_ref[clip * count:(clip + 1) * count, :]
        gram_ref[clip] = lax.dot_general(own, own, ROWS, preferred_element_type=F32)
    loads[4].wait()
    keys = lax.dot_general(rows_ref[...], query_weight[...], ROWS, preferred_element_type=F32)
    key_ref[...] = (keys * scale).astype(BF16)


def score_kernel(
    place_ref, counts_ref, pos_ref, text_ref, key_ref, value_ref, gram_ref,
    similar_ref, loss_ref, terms_ref,
):
    clips, frames = gram_ref.shape[0], gram_ref.shape[1]
    texts = text_ref.shape[0]
    block = texts // (2 * PAIR)
    place = place_ref[0]
    text = text_ref[...]
    scores = lax.dot_general(key_ref[...], text, ROWS, preferred_element_type=F32)
    inner_all = lax.dot_general(value_ref[...], text, ROWS, preferred_element_type=F32)
    text_wide = text.astype(F32)
    sq_high, sq_low = split_bf16(text_wide * text_wide)
    ones = jnp.ones((8, text.shape[1]), BF16)
    text_sq = lax.dot_general(ones, sq_high, ROWS, preferred_element_type=F32)
    text_sq = (text_sq + lax.dot_general(ones, sq_low, ROWS, preferred_element_type=F32))[:1]
    frame_index = lax.broadcasted_iota(jnp.int32, (frames, texts), 0)
    clip_index = lax.broadcasted_iota(jnp.int32, (clips, texts), 0)
    inner = jnp.zeros((clips, texts), F32)
    pooled_sq = jnp.zeros((clips, texts), F32)
    position = jnp.zeros((clips, texts), jnp.int32)
    for clip in range(clips):
        rows = slice(clip * frames, (clip + 1) * frames)
        valid = frame_index < counts_ref[clip]
        score = jnp.where(valid, scores[rows], -jnp.inf)
        weights = jnp.exp(score - jnp.max(score, axis=0, keepdims=True))
        weights = weights * (1.0 / jnp.sum(weights, axis=0, keepdims=True))
        w_high, w_low = split_bf16(weights)
        g_high, g_low = split_bf16(gram_ref[clip])
        mixed = (
            jnp.dot(g_high, w_high, preferred_element_type=F32)
            + jnp.dot(g_high, w_low, preferred_element_type=F32)
            + jnp.dot(g_low, w_high, preferred_element_type=F32)
        )
        here = clip_index == clip
        inner = jnp.where(here, jnp.sum(weights * inner_all[rows], axis=0, keepdims=True), inner)
        pooled_sq = jnp.where(here, jnp.sum(weights * mixed, axis=0, keepdims=True), pooled_sq)
        position = jnp.where(here, pos_ref[clip], position)
    pooled_sq = jnp.maximum(pooled_sq, 0.0)
    similar = LOGIT_SCALE * inner / jnp.sqrt((pooled_sq + EPSILON) * (text_sq + EPSILON))
    lane = lax.broadcasted_iota(jnp.int32, (clips, texts), 1)
    older = lane // SLICE % 2
    bringer = lane // (2 * block)
    hop = place + jnp.where(older == 1, bringer + 1, -bringer)
    in_block = lane // (2 * SLICE) * SLICE % block + lane % SLICE
    exp_sims = jnp.where((hop >= 0) & (hop <= HOPS), jnp.exp(similar), 0.0)
    terms_ref[...] = jnp.broadcast_to(jnp.sum(exp_sims, axis=0, keepdims=True)[None], terms_ref.shape)
    similar_ref[...] = similar
    hit = (hop >= 0) & (hop <= HOPS) & (hop * block + in_block == position)
    picked = jnp.sum(jnp.where(hit, similar, 0.0), axis=1, keepdims=True)
    total = jnp.sum(exp_sims, axis=1, keepdims=True)
    loss_ref[...] = jnp.broadcast_to(jnp.log(total) - picked, loss_ref.shape)


def local(frames, texts, w_query, w_key, w_value, w_out, frame_counts, clip_pos):
    clips, frame_total, width = frames.shape
    slice_rows = texts.shape[0]
    tm_count = lax.axis_size("tm")
    dp_count = lax.axis_size("dp")
    groups = block_groups(dp_count, tm_count, PAIR)
    peers = PAIR * tm_count
    block_rows = slice_rows * tm_count
    place = lax.axis_index("dp") % PAIR

    outgoing = lax.optimization_barrier(jnp.broadcast_to(texts[None, None], (peers, 2, slice_rows, width)))
    crossed = [(source, (source + (1 if source % PAIR else 3)) % dp_count) for source in range(dp_count)]
    before = lax.ppermute(texts, "dp", crossed)
    before = jnp.broadcast_to(before[None, None], (peers, 1, slice_rows, width))
    outgoing = lax.dynamic_update_slice(outgoing, before, (0, 1, 0, 0))
    band_text = lax.all_to_all(
        outgoing.reshape(peers, 2 * slice_rows, width),
        BOTH, 0, 0, axis_index_groups=groups, tiled=True,
    ).reshape(2 * peers * slice_rows, width)

    smem = pl.BlockSpec(memory_space=pltpu.SMEM)
    vmem = pl.BlockSpec(memory_space=pltpu.VMEM)
    rows = clips * frame_total
    key_rows, value_rows, gram = pl.pallas_call(
        project_kernel,
        in_specs=[pl.BlockSpec(memory_space=pltpu.HBM)] * 5,
        out_specs=[vmem] * 3,
        out_shape=[
            jax.ShapeDtypeStruct((rows, width), BF16),
            jax.ShapeDtypeStruct((rows, width), BF16),
            jax.ShapeDtypeStruct((clips, frame_total, frame_total), F32),
        ],
        scratch_shapes=[
            pltpu.VMEM((rows, width), BF16),
            *[pltpu.VMEM((width, width), BF16)] * 4,
            pltpu.VMEM((rows, width), BF16),
            pltpu.SemaphoreType.DMA((5,)),
        ],
        compiler_params=pltpu.CompilerParams(vmem_limit_bytes=52 * 1024 * 1024),
        cost_estimate=pl.CostEstimate(
            flops=8 * rows * width * width, bytes_accessed=8 * width * width, transcendentals=0
        ),
    )(frames.reshape(rows, width), w_key, w_query, w_value, w_out)

    similar, loss, terms = pl.pallas_call(
        score_kernel,
        in_specs=[smem] * 3 + [vmem] * 4,
        out_specs=[vmem] * 3,
        out_shape=[
            jax.ShapeDtypeStruct((clips, 2 * peers * slice_rows), F32),
            jax.ShapeDtypeStruct((clips, 128), F32),
            jax.ShapeDtypeStruct((RING * tm_count, 1, 2 * peers * slice_rows), F32),
        ],
        compiler_params=pltpu.CompilerParams(vmem_limit_bytes=24 * 1024 * 1024),
        cost_estimate=pl.CostEstimate(flops=500_000_000, bytes_accessed=3_000_000, transcendentals=120_000),
    )(place.reshape(1), frame_counts, clip_pos, band_text, key_rows, value_rows, gram)

    met = lax.all_to_all(
        terms, BOTH, 0, 0, axis_index_groups=block_groups(dp_count, tm_count, RING), tiled=True
    )
    met = jnp.sum(met.reshape(RING // PAIR, peers, -1), axis=1)
    mine = lax.axis_index("tm") * 2 * slice_rows
    half = 2 * block_rows
    newer = lax.dynamic_slice_in_dim(met, place * half + mine, slice_rows, axis=1)
    older = lax.dynamic_slice_in_dim(met, (1 - place) * half + mine + slice_rows, slice_rows, axis=1)
    later = lax.axis_index("dp") % RING >= PAIR
    newer = jnp.where(later, newer[1], newer[0])
    older = jnp.where(later, older[0], older[1])
    similar, loss, older = lax.optimization_barrier((similar, loss, older))
    beyond = moved(older, -RING, range(PAIR, RING))
    text_lse = jnp.log(newer + jnp.where(later, beyond, older))

    similar = similar.reshape(clips, PAIR, tm_count, 2, slice_rows)

    def part(which, older):
        return similar[:, which, :, older, :].reshape(clips, block_rows)

    first = place == 0
    by_hop = [
        jnp.where(first, part(0, 0), part(1, 0)),
        jnp.where(first, part(0, 1), part(0, 0)),
        jnp.where(first, part(1, 1), part(0, 1)),
    ]
    return (jnp.stack(by_hop, axis=1), loss[:, 0], text_lse)


def solution(mesh):
    in_specs = (
        P(BOTH, None, None), P(BOTH, None), P(), P(), P(), P(), P(BOTH), P(BOTH),
    )
    out_specs = (P(BOTH, None, None), P(BOTH), P(BOTH))
    return jax.shard_map(local, mesh=mesh, in_specs=in_specs, out_specs=out_specs, check_vma=False)
```

```python
import jax
import jax.numpy as jnp
from jax import lax
from jax.experimental import pallas as pl
from jax.experimental.pallas import tpu as pltpu
from jax.sharding import PartitionSpec as P

HOPS = 2
RING = 4
PAIR = 2
LOGIT_SCALE = 32.0
EPSILON = 1e-06
SLICE = 8
BOTH = ("dp", "tm")
F32 = jnp.float32
BF16 = jnp.bfloat16
ROWS = (((1,), (1,)), ((), ()))


def block_groups(dp_count, tm_count, blocks):
    width = blocks * tm_count
    return [list(range(g * width, (g + 1) * width)) for g in range(dp_count // blocks)]


def moved(value, blocks, places=range(RING)):
    count = lax.axis_size("dp")
    pairs = [(source, (source + blocks) % count) for source in range(count) if source % RING in places]
    return lax.ppermute(value, "dp", pairs)


def split_bf16(value):
    high = value.astype(BF16)
    return high, (value - high.astype(F32)).astype(BF16)


def project_kernel(
    frames_hbm, key_hbm, query_hbm, value_hbm, out_hbm,
    key_ref, value_ref, gram_ref,
    frames_ref, value_weight, out_weight, key_weight, query_weight, rows_ref, sems,
):
    clips, count = gram_ref.shape[0], gram_ref.shape[1]
    scale = frames_ref.shape[1] ** -0.5
    loads = [
        pltpu.make_async_copy(source, held, sems.at[at])
        for at, (source, held) in enumerate((
            (frames_hbm, frames_ref), (value_hbm, value_weight), (out_hbm, out_weight),
            (key_hbm, key_weight), (query_hbm, query_weight),
        ))
    ]
    for load in loads:
        load.start()
    loads[0].wait()
    loads[1].wait()
    rows_ref[...] = jnp.dot(frames_ref[...], value_weight[...], preferred_element_type=F32).astype(BF16)
    loads[2].wait()
    value_ref[...] = jnp.dot(rows_ref[...], out_weight[...], preferred_element_type=F32).astype(BF16)
    loads[3].wait()
    rows_ref[...] = jnp.dot(frames_ref[...], key_weight[...], preferred_element_type=F32).astype(BF16)
    for clip in range(clips):
        own = value_ref[clip * count:(clip + 1) * count, :]
        gram_ref[clip] = lax.dot_general(own, own, ROWS, preferred_element_type=F32)
    loads[4].wait()
    keys = lax.dot_general(rows_ref[...], query_weight[...], ROWS, preferred_element_type=F32)
    key_ref[...] = (keys * scale).astype(BF16)


def score_kernel(
    place_ref, counts_ref, pos_ref, text_ref, key_ref, value_ref, gram_ref,
    similar_ref, loss_ref, terms_ref,
):
    clips, frames = gram_ref.shape[0], gram_ref.shape[1]
    texts = text_ref.shape[0]
    block = texts // (2 * PAIR)
    place = place_ref[0]
    text = text_ref[...]
    scores = lax.dot_general(key_ref[...], text, ROWS, preferred_element_type=F32)
    inner_all = lax.dot_general(value_ref[...], text, ROWS, preferred_element_type=F32)
    text_wide = text.astype(F32)
    sq_high, sq_low = split_bf16(text_wide * text_wide)
    ones = jnp.ones((8, text.shape[1]), BF16)
    text_sq = lax.dot_general(ones, sq_high, ROWS, preferred_element_type=F32)
    text_sq = (text_sq + lax.dot_general(ones, sq_low, ROWS, preferred_element_type=F32))[:1]
    frame_index = lax.broadcasted_iota(jnp.int32, (frames, texts), 0)
    clip_index = lax.broadcasted_iota(jnp.int32, (clips, texts), 0)
    inner = jnp.zeros((clips, texts), F32)
    pooled_sq = jnp.zeros((clips, texts), F32)
    position = jnp.zeros((clips, texts), jnp.int32)
    for clip in range(clips):
        rows = slice(clip * frames, (clip + 1) * frames)
        valid = frame_index < counts_ref[clip]
        score = jnp.where(valid, scores[rows], -jnp.inf)
        weights = jnp.exp(score - jnp.max(score, axis=0, keepdims=True))
        weights = weights * (1.0 / jnp.sum(weights, axis=0, keepdims=True))
        w_high, w_low = split_bf16(weights)
        g_high, g_low = split_bf16(gram_ref[clip])
        mixed = (
            jnp.dot(g_high, w_high, preferred_element_type=F32)
            + jnp.dot(g_high, w_low, preferred_element_type=F32)
            + jnp.dot(g_low, w_high, preferred_element_type=F32)
        )
        here = clip_index == clip
        inner = jnp.where(here, jnp.sum(weights * inner_all[rows], axis=0, keepdims=True), inner)
        pooled_sq = jnp.where(here, jnp.sum(weights * mixed, axis=0, keepdims=True), pooled_sq)
        position = jnp.where(here, pos_ref[clip], position)
    pooled_sq = jnp.maximum(pooled_sq, 0.0)
    similar = LOGIT_SCALE * inner / jnp.sqrt((pooled_sq + EPSILON) * (text_sq + EPSILON))
    lane = lax.broadcasted_iota(jnp.int32, (clips, texts), 1)
    older = lane // SLICE % 2
    bringer = lane // (2 * block)
    hop = place + jnp.where(older == 1, bringer + 1, -bringer)
    in_block = lane // (2 * SLICE) * SLICE % block + lane % SLICE
    exp_sims = jnp.where((hop >= 0) & (hop <= HOPS), jnp.exp(similar), 0.0)
    terms_ref[...] = jnp.broadcast_to(jnp.sum(exp_sims, axis=0, keepdims=True)[None], terms_ref.shape)
    similar_ref[...] = similar
    hit = (hop >= 0) & (hop <= HOPS) & (hop * block + in_block == position)
    picked = jnp.sum(jnp.where(hit, similar, 0.0), axis=1, keepdims=True)
    total = jnp.sum(exp_sims, axis=1, keepdims=True)
    loss = jnp.log(total) - picked
    square = (clips, clips)
    same = lax.broadcasted_iota(jnp.int32, square, 0) == lax.broadcasted_iota(jnp.int32, square, 1)
    loss_ref[...] = jnp.sum(jnp.where(same, loss, 0.0), axis=0, keepdims=True)


def local(frames, texts, w_query, w_key, w_value, w_out, frame_counts, clip_pos):
    clips, frame_total, width = frames.shape
    slice_rows = texts.shape[0]
    tm_count = lax.axis_size("tm")
    dp_count = lax.axis_size("dp")
    groups = block_groups(dp_count, tm_count, PAIR)
    peers = PAIR * tm_count
    block_rows = slice_rows * tm_count
    place = lax.axis_index("dp") % PAIR

    outgoing = lax.optimization_barrier(jnp.broadcast_to(texts[None, None], (peers, 2, slice_rows, width)))
    crossed = [(source, (source + (1 if source % PAIR else 3)) % dp_count) for source in range(dp_count)]
    before = lax.ppermute(texts, "dp", crossed)
    before = jnp.broadcast_to(before[None, None], (peers, 1, slice_rows, width))
    outgoing = lax.dynamic_update_slice(outgoing, before, (0, 1, 0, 0))
    band_text = lax.all_to_all(
        outgoing.reshape(peers, 2 * slice_rows, width),
        BOTH, 0, 0, axis_index_groups=groups, tiled=True,
    ).reshape(2 * peers * slice_rows, width)

    smem = pl.BlockSpec(memory_space=pltpu.SMEM)
    vmem = pl.BlockSpec(memory_space=pltpu.VMEM)
    rows = clips * frame_total
    key_rows, value_rows, gram = pl.pallas_call(
        project_kernel,
        in_specs=[pl.BlockSpec(memory_space=pltpu.HBM)] * 5,
        out_specs=[vmem] * 3,
        out_shape=[
            jax.ShapeDtypeStruct((rows, width), BF16),
            jax.ShapeDtypeStruct((rows, width), BF16),
            jax.ShapeDtypeStruct((clips, frame_total, frame_total), F32),
        ],
        scratch_shapes=[
            pltpu.VMEM((rows, width), BF16),
            *[pltpu.VMEM((width, width), BF16)] * 4,
            pltpu.VMEM((rows, width), BF16),
            pltpu.SemaphoreType.DMA((5,)),
        ],
        compiler_params=pltpu.CompilerParams(vmem_limit_bytes=52 * 1024 * 1024),
        cost_estimate=pl.CostEstimate(
            flops=8 * rows * width * width, bytes_accessed=8 * width * width, transcendentals=0
        ),
    )(frames.reshape(rows, width), w_key, w_query, w_value, w_out)

    similar, loss, terms = pl.pallas_call(
        score_kernel,
        in_specs=[smem] * 3 + [vmem] * 4,
        out_specs=[vmem] * 3,
        out_shape=[
            jax.ShapeDtypeStruct((clips, 2 * peers * slice_rows), F32),
            jax.ShapeDtypeStruct((1, clips), F32),
            jax.ShapeDtypeStruct((RING * tm_count, 1, 2 * peers * slice_rows), F32),
        ],
        compiler_params=pltpu.CompilerParams(vmem_limit_bytes=24 * 1024 * 1024),
        cost_estimate=pl.CostEstimate(flops=500_000_000, bytes_accessed=3_000_000, transcendentals=120_000),
    )(place.reshape(1), frame_counts, clip_pos, band_text, key_rows, value_rows, gram)

    similar, loss, terms = lax.optimization_barrier((similar, loss, terms))
    met = lax.all_to_all(
        terms, BOTH, 0, 0, axis_index_groups=block_groups(dp_count, tm_count, RING), tiled=True
    )
    met = jnp.sum(met.reshape(RING // PAIR, peers, -1), axis=1)
    mine = lax.axis_index("tm") * 2 * slice_rows
    half = 2 * block_rows
    newer = lax.dynamic_slice_in_dim(met, place * half + mine, slice_rows, axis=1)
    older = lax.dynamic_slice_in_dim(met, (1 - place) * half + mine + slice_rows, slice_rows, axis=1)
    later = lax.axis_index("dp") % RING >= PAIR
    newer = jnp.where(later, newer[1], newer[0])
    older = jnp.where(later, older[0], older[1])
    beyond = moved(older, -RING, range(PAIR, RING))
    text_lse = jnp.log(newer + jnp.where(later, beyond, older))

    similar = similar.reshape(clips, PAIR, tm_count, 2, slice_rows)

    def part(which, older):
        return similar[:, which, :, older, :].reshape(clips, block_rows)

    first = place == 0
    by_hop = [
        jnp.where(first, part(0, 0), part(1, 0)),
        jnp.where(first, part(0, 1), part(0, 0)),
        jnp.where(first, part(1, 1), part(0, 1)),
    ]
    return (jnp.stack(by_hop, axis=1), loss.reshape(clips), text_lse)


def solution(mesh):
    in_specs = (
        P(BOTH, None, None), P(BOTH, None), P(), P(), P(), P(), P(BOTH), P(BOTH),
    )
    out_specs = (P(BOTH, None, None), P(BOTH), P(BOTH))
    return jax.shard_map(local, mesh=mesh, in_specs=in_specs, out_specs=out_specs, check_vma=False)
```
